32 devices in a mesh: teacher: 4 (over y, x), dp: 2 (over core), vocab: 4 (over z).
Axes of the slice: x: 2, y: 2, z: 4, core: 2. Of those that a mesh axis runs over, the one named last changes fastest.
Arguments:
- teacher_of_seq: int32 [16], replicated, may hold values from 0 to 3, as said below
- teacher_hidden: bfloat16 [4, 512, 4096], P('teacher', 'vocab', 'dp'), may hold values from -160 to 160, as said below
- teacher_weight: bfloat16 [4, 4096, 8192], P('teacher', 'dp', 'vocab'), may hold values from -0.09375 to 0.09375
- student_hidden: bfloat16 [1024, 3072], P(None, ('teacher', 'dp')), may hold values from -160 to 160
- student_weight: bfloat16 [3072, 8192], P(('teacher', 'dp'), 'vocab'), may hold values from -0.109375 to 0.109375
Outputs:
- kl_rows: float32 [1024], P(('teacher', 'dp'))
- grad_weight: bfloat16 [3072, 8192], P(('teacher', 'dp'), 'vocab')
- grad_hidden: bfloat16 [1024, 3072], P('vocab', ('teacher', 'dp'))
The draws below stay inside these ranges and needn't reach their ends.
Inputs may be any that keep to these rules, and one draw needn't show every extreme that they name: `teacher_of_seq`: every teacher has at least one sequence and one teacher has exactly 8. `teacher_hidden`: slots from 64 times the teacher's number of sequences on are not read.
All inputs are finite; a program needn't handle non-finite values.
Results may differ from the reference program's by a relative error of at most 0.01225.
The reference program's roundings to bfloat16 on the way (of `teacher_logits` and `grad_logits`) count: a program that leaves them out, or rounds other values in their place, can miss the bound.
Values may be sent and summed in bfloat16 or wider, within the bound.
A program may use at most 128 MiB of HBM per device.

```python
import jax
import jax.numpy as jnp
from jax import lax

SEQS = 16
POS = 64
TD = 4096
SD = 3072
TEACHERS = 4
CAP = 512
ROWS = 1024
VOCAB = 8192


def draw_teacher_of_seq(key, part):
    half = SEQS // 2
    hottest = jax.random.randint(jax.random.fold_in(key, 11), (), 0, TEACHERS)
    cuts = jnp.sort(jax.random.permutation(jax.random.fold_in(key, 12), half - 1)[:2] + 1)
    others = jnp.stack([cuts[0], cuts[1] - cuts[0], half - cuts[1]]).astype(jnp.int32)
    teacher_ids = jnp.arange(TEACHERS, dtype=jnp.int32)
    ranked = jnp.clip(teacher_ids - (teacher_ids > hottest).astype(jnp.int32), 0, 2)
    counts = jnp.where(teacher_ids == hottest, half, others[ranked]).astype(jnp.int32)
    ends = jnp.cumsum(counts)
    sequence = jnp.arange(SEQS, dtype=jnp.int32)
    labels = jnp.sum((sequence[:, None] >= ends[None, :]).astype(jnp.int32), axis=1).astype(jnp.int32)
    pick = jax.random.randint(jax.random.fold_in(key, 13), (), 0, 2).astype(jnp.int32)
    target = ((pick + 2) % TEACHERS).astype(jnp.int32)
    first = (pick * (SEQS // 4)).astype(jnp.int32)
    scores = jax.random.permutation(jax.random.fold_in(key, 14), SEQS).astype(jnp.int32)
    is_target = labels == target
    smaller = scores[None, :] < scores[:, None]
    rank_other = jnp.sum((smaller & jnp.logical_not(is_target)[None, :]).astype(jnp.int32), axis=1)
    rank_target = jnp.sum((smaller & is_target[None, :]).astype(jnp.int32), axis=1)
    leading = is_target & (rank_target == 0)
    placed = jnp.logical_not(is_target) & (rank_other < first)
    sort_keys = jnp.where(placed, rank_other, jnp.where(leading, first, SEQS + scores)).astype(jnp.int32)
    order = jnp.argsort(sort_keys, stable=True)
    return labels[order].astype(jnp.int32)


def scaled_rows(key, shape):
    values = jnp.clip(jax.random.normal(jax.random.fold_in(key, 21), shape, jnp.float32), -4.0, 4.0)
    return values


def draw_teacher_hidden(key, part):
    return scaled_rows(key, (TEACHERS, CAP, TD)).astype(jnp.bfloat16)


def draw_student_hidden(key, part):
    return scaled_rows(jax.random.fold_in(key, 31), (ROWS, SD)).astype(jnp.bfloat16)


def levels(stream_key, dims, shards, least, high):
    factor_of = 1.0
    for axis_at, parts in shards:
        heights = jax.random.uniform(jax.random.fold_in(jax.random.fold_in(stream_key, 6), axis_at), (parts,), jnp.float32, least / len(shards), high / len(shards))
        factor_of = factor_of * jnp.repeat(jnp.exp(heights), dims[axis_at] // parts).reshape((-1,) + (1,) * (len(dims) - 1 - axis_at))
    return factor_of


def gaussian(rng, dims, deviation, limit, shards=(), kind=jnp.bfloat16):
    level = levels(rng, dims, shards, -0.22, 0.18) if shards else 1.0
    array = jax.random.normal(rng, dims, jnp.float32) * deviation * level
    return jnp.minimum(jnp.maximum(array, -limit), limit).astype(kind)


def setup_inputs(seed: int = 0) -> dict:
    keys = jax.random.split(jax.random.key(seed), 6)
    return {
        "teacher_of_seq": draw_teacher_of_seq(jax.random.fold_in(keys[5], 71), 0),
        "teacher_hidden": draw_teacher_hidden(jax.random.fold_in(keys[5], 71), 0),
        "teacher_weight": gaussian(keys[2], (TEACHERS, TD, VOCAB), TD ** -0.5, 0.09375, ((0, 4), (1, 2), (2, 4))),
        "student_hidden": draw_student_hidden(jax.random.fold_in(keys[5], 71), 0),
        "student_weight": gaussian(keys[4], (SD, VOCAB), SD ** -0.5, 0.109375, ((0, 8), (1, 4))),
    }


def head_rows(pair):
    hidden, weight = pair
    return jnp.dot(hidden, weight, preferred_element_type=jnp.float32).astype(jnp.bfloat16)


def row_lse(logits):
    row_max = jnp.max(logits, axis=1)
    total = jnp.sum(jnp.exp(logits - row_max[:, None]), axis=1)
    return row_max + jnp.log(total)


def reference(teacher_of_seq, teacher_hidden, teacher_weight, student_hidden, student_weight):
    sequence_ids = jnp.arange(SEQS, dtype=jnp.int32)
    same_before = (teacher_of_seq[None, :] == teacher_of_seq[:, None]) & (sequence_ids[None, :] < sequence_ids[:, None])
    earlier = jnp.sum(same_before.astype(jnp.int32), axis=1).astype(jnp.int32)
    row_teacher = jnp.repeat(teacher_of_seq, POS).astype(jnp.int32)
    within = (jnp.arange(ROWS, dtype=jnp.int32) % POS).astype(jnp.int32)
    slot_index = (jnp.repeat(earlier, POS) * POS + within).astype(jnp.int32)
    slot_logits = lax.map(head_rows, (teacher_hidden, teacher_weight))
    teacher_logits = slot_logits[row_teacher, slot_index].astype(jnp.float32)
    student_logits = jnp.dot(student_hidden, student_weight, preferred_element_type=jnp.float32)
    teacher_lse = row_lse(teacher_logits)
    student_lse = row_lse(student_logits)
    teacher_prob = jnp.exp(teacher_logits - teacher_lse[:, None])
    cross_term = jnp.sum(teacher_prob * (teacher_logits - student_logits), axis=1)
    kl_rows = cross_term - teacher_lse + student_lse
    grad_logits = (VOCAB * (jnp.exp(student_logits - student_lse[:, None]) - teacher_prob)).astype(jnp.bfloat16)
    grad_weight = jnp.dot(student_hidden.T, grad_logits, preferred_element_type=jnp.float32).astype(jnp.bfloat16)
    grad_hidden = jnp.dot(grad_logits, student_weight.T, preferred_element_type=jnp.float32).astype(jnp.bfloat16)
    return (kl_rows, grad_weight, grad_hidden)
```

```python
import functools

import jax
import jax.numpy as jnp
from jax import lax
from jax.experimental import pallas as pl
from jax.experimental.pallas import tpu as pltpu
from jax.sharding import PartitionSpec as P

MESH = pl.DeviceIdType.MESH
F32 = jnp.float32
BF16 = jnp.bfloat16


def kernel(
    Z, vocab_total,
    pick_ref, hidden_ref, head_ref, x_ref, w_ref,
    kl_ref, gw_ref, gh_ref,
    head, th, ph, work, s_rx, s_r1, s_r2, t_rx, t_sum, t_r1, t_r2, xt, st, tile, g_all, ghp, gh_rx,
    head_sem, z_send, z_recv,
    sc_send, sc_recv, s1_send, s1_recv, s2_send, s2_recv,
    tc_send, tc_recv, t1_send, t1_recv, t2_send, t2_recv,
    st_send, st_recv, g_send, g_recv, gc_send, gc_recv, gh_send, gh_recv,
):
    t = lax.axis_index("teacher")
    c = lax.axis_index("dp")
    z = lax.axis_index("vocab")
    low = lax.rem(t, 2)
    high = lax.div(t, 2)
    mates = (t, t + 1 - 2 * low, t + 2 - 4 * high, 3 - t)
    other = 1 - c
    devs = tuple((m, c, z) for m in mates)
    core = (t, other, z)
    rows, cols = s_r2.shape
    half = cols // 2
    cut = (pl.ds(0, half), pl.ds(half, half))
    zrows = hidden_ref.shape[0]
    hrows = gh_ref.shape[0]

    def at(block, count):
        return pl.ds(pl.multiple_of(block * count, count), count)

    def remote(src, dst, send, recv, dev):
        return pltpu.make_async_remote_copy(
            src_ref=src, dst_ref=dst, send_sem=send, recv_sem=recv, device_id=dev, device_id_type=MESH
        )

    barrier = pltpu.get_barrier_semaphore()
    for dev in (core, devs[1], devs[2]):
        pl.semaphore_signal(barrier, inc=1, device_id=dev, device_id_type=MESH)
    for dz in range(1, Z):
        pl.semaphore_signal(barrier, inc=1, device_id=(t, c, lax.rem(z + dz, Z)), device_id_type=MESH)
    head_copy = pltpu.make_async_copy(head_ref, head, head_sem)
    head_copy.start()
    th[at(z, zrows), :] = hidden_ref[...]
    pl.semaphore_wait(barrier, 2 + Z)

    def z_copy(block, way, step, target):
        return remote(
            th.at[at(block, zrows)], th.at[at(block, zrows)], z_send.at[way, step], z_recv.at[block], (t, c, target)
        )

    def z_start(step):
        @pl.when((z - step >= 0) & (z + 1 < Z))
        def _():
            z_copy(z - step, 0, step, z + 1).start()

        @pl.when((z + step < Z) & (z >= 1))
        def _():
            z_copy(z + step, 1, step, z - 1).start()

    def z_wait(step):
        @pl.when(z - 1 - step >= 0)
        def _():
            z_copy(z - 1 - step, 0, step, z - 1).wait_recv()

        @pl.when(z + 1 + step < Z)
        def _():
            z_copy(z + 1 + step, 1, step, z + 1).wait_recv()

    def z_end(step):
        @pl.when((z - step >= 0) & (z + 1 < Z))
        def _():
            z_copy(z - step, 0, step, z + 1).wait_send()

        @pl.when((z + step < Z) & (z >= 1))
        def _():
            z_copy(z + step, 1, step, z - 1).wait_send()

    def owner(j, which):
        return 2 * mates[j] + which

    def first_hop(j, summed, r1, sems):
        send, recv = sems
        copies = []
        if j == 3:
            for h in (0, 1):
                copies.append(
                    remote(summed.at[3, :, cut[h]], r1.at[0, :, cut[h]], send.at[0, h], recv.at[0, h], devs[1 + h])
                )
        elif j in (1, 2):
            h = j - 1
            copies.append(
                remote(summed.at[j, :, cut[h]], r1.at[1, :, cut[h]], send.at[1, h], recv.at[1, h], devs[j])
            )
        for copy in copies:
            copy.start()
        return copies

    def second_hop(h, first, summed, r1, r2, sems):
        send, recv = sems
        j = 2 - h
        first[h].wait_recv()
        summed[j, :, cut[h]] = (
            summed[j, :, cut[h]].astype(F32) + r1[0, :, cut[h]].astype(F32)
        ).astype(summed.dtype)
        copy = remote(summed.at[j, :, cut[h]], r2.at[:, cut[h]], send.at[h], recv.at[h], devs[j])
        copy.start()
        return copy

    ORDER = (3, 1, 2, 0)
    z_start(0)
    pair = {}
    for j in ORDER:
        work[j, other] = jnp.dot(x_ref[at(owner(j, other), rows), :], w_ref[...], preferred_element_type=F32)
        pair[j] = remote(work.at[j, other], s_rx.at[j], sc_send.at[j], sc_recv.at[j], core)
        pair[j].start()
    s_first = []
    for j in ORDER:
        mine = jnp.dot(x_ref[at(owner(j, c), rows), :], w_ref[...], preferred_element_type=F32)
        pair[j].wait_recv()
        s_rx[j] = s_rx[j] + mine
        s_first += first_hop(j, s_rx, s_r1, (s1_send, s1_recv))
    xt[...] = x_ref[...].T
    for step in range(Z - 1):
        z_wait(step)
        if step + 1 < Z - 1:
            z_start(step + 1)
        if step == 0:
            s_second = [second_hop(h, s_first, s_rx, s_r1, s_r2, (s2_send, s2_recv)) for h in (0, 1)]
    head_copy.wait()

    for j in ORDER:
        pair[j].wait_send()
    chunk = cols // 8
    tpair = {}
    for j in ORDER:
        ph[...] = jnp.dot(
            pick_ref[at(mates[j], 2 * rows), :], th[...], preferred_element_type=F32
        ).astype(BF16)

        @pl.loop(0, 8)
        def _(i, j=j):
            where = at(i, chunk)
            part = jnp.dot(ph[...], head[:, where], preferred_element_type=F32)
            work[j, 0, :, where] = part[:rows]
            work[j, 1, :, where] = part[rows:]

        tpair[j] = remote(work.at[j, other], t_rx.at[j], tc_send.at[j], tc_recv.at[j], core)
        tpair[j].start()
    t_first = []
    for j in ORDER:
        tpair[j].wait_recv()
        t_sum[j] = (t_rx[j] + work[j, c]).astype(BF16)
        t_first += first_hop(j, t_sum, t_r1, (t1_send, t1_recv))
    t_second = [second_hop(h, t_first, t_sum, t_r1, t_r2, (t2_send, t2_recv)) for h in (0, 1)]

    s_first[2].wait_recv()
    s_first[3].wait_recv()
    for h in (0, 1):
        s_second[h].wait_recv()
    s_rx[0] = s_rx[0] + s_r1[1] + s_r2[...]
    student = s_rx[0]
    s_top = jnp.max(student, axis=1, keepdims=True)
    s_total = jnp.sum(jnp.exp(student - s_top), axis=1, keepdims=True)
    t_first[2].wait_recv()
    t_first[3].wait_recv()
    for h in (0, 1):
        t_second[h].wait_recv()
    t_sum[0] = (t_sum[0].astype(F32) + t_r1[1].astype(F32) + t_r2[...].astype(F32)).astype(BF16)
    teacher = t_sum[0].astype(F32)
    t_top = jnp.max(teacher, axis=1, keepdims=True)
    t_exp = jnp.exp(teacher - t_top)
    t_total = jnp.sum(t_exp, axis=1, keepdims=True)
    cross = jnp.sum(t_exp * (teacher - s_rx[0]), axis=1, keepdims=True)
    lane = lax.broadcasted_iota(jnp.int32, tile.shape, 1)
    packed = jnp.zeros(tile.shape, F32)
    for k, column in enumerate((t_top, t_total, s_top, s_total, cross)):
        packed = jnp.where(lane == k, column, packed)
    st[z] = packed.T[:8, :]
    st_out = []
    for dz in range(1, Z):
        copy = remote(st.at[z], st.at[z], st_send.at[dz], st_recv.at[z], (t, c, lax.rem(z + dz, Z)))
        copy.start()
        st_out.append(copy)
    for dz in range(1, Z):
        source = lax.rem(z + dz, Z)
        remote(st.at[source], st.at[source], st_send.at[dz], st_recv.at[source], (t, c, source)).wait_recv()
    every = [st[k] for k in range(Z)]
    t_top = functools.reduce(jnp.maximum, [e[0:1] for e in every])
    s_top = functools.reduce(jnp.maximum, [e[2:3] for e in every])
    t_total = sum(e[1:2] * jnp.exp(e[0:1] - t_top) for e in every)
    s_total = sum(e[3:4] * jnp.exp(e[2:3] - s_top) for e in every)
    t_lse = t_top + jnp.log(t_total)
    s_lse = s_top + jnp.log(s_total)
    cross = sum(e[4:5] * jnp.exp(e[0:1] - t_lse) for e in every)
    kl = cross - t_lse + s_lse
    kl_ref[...] = jnp.broadcast_to(kl, kl_ref.shape)
    line = lax.broadcasted_iota(jnp.int32, tile.shape, 0)
    tile[...] = jnp.where(line == 0, t_lse, jnp.where(line == 1, s_lse, 0.0)).T
    t_lse = tile[:, 0:1]
    s_lse = tile[:, 1:2]
    me = owner(0, c)
    g_all[at(me, rows), :] = (
        vocab_total * (jnp.exp(s_rx[0] - s_lse) - jnp.exp(t_sum[0].astype(F32) - t_lse))
    ).astype(BF16)

    def g_copy(j, which, sems, k, dev, columns=pl.ds(0, cols)):
        ref = g_all.at[at(owner(j, which), rows), columns]
        return remote(ref, ref, sems[0].at[k], sems[1].at[k], dev)

    chips, cores = (g_send, g_recv), (gc_send, gc_recv)
    sent = [g_copy(0, c, chips, 0, devs[1]), g_copy(0, c, chips, 1, devs[2]), g_copy(0, c, cores, 0, core)]
    for copy in sent:
        copy.start()

    def arrived(j, k, columns=pl.ds(0, cols)):
        g_copy(j, c, chips, k, devs[1], columns).wait_recv()

    def forward(j, sems, k, dev, columns=pl.ds(0, cols)):
        copy = g_copy(j, c, sems, k, dev, columns)
        copy.start()
        sent.append(copy)

    gh_out = []

    def hidden_rows(j):
        g_copy(j, other, cores, j, core).wait_recv()
        where = at(mates[j], 2 * rows)
        ghp[where, :] = lax.dot_general(
            g_all[where, :], w_ref[...], (((1,), (1,)), ((), ())), preferred_element_type=F32
        ).astype(BF16)
        for q in range(Z // 4):
            target = mates[j] * (Z // 4) + q
            copy = remote(
                ghp.at[at(target, hrows)], gh_rx.at[z], gh_send.at[j * (Z // 4) + q], gh_recv.at[z], (t, c, target)
            )
            gh_out.append((target, copy))

            @pl.when(target != z)
            def _(copy=copy):
                copy.start()

    arrived(1, 0)
    forward(1, chips, 2, devs[2], cut[0])
    forward(1, cores, 1, core)
    arrived(2, 1)
    forward(2, chips, 3, devs[1], cut[1])
    forward(2, cores, 2, core)
    hidden_rows(0)
    hidden_rows(1)
    hidden_rows(2)
    arrived(3, 2, cut[0])
    arrived(3, 3, cut[1])
    forward(3, cores, 3, core)
    hidden_rows(3)

    wide = cols // 4
    @pl.loop(0, 4)
    def _(i):
        where = at(i, wide)
        gw_ref[:, where] = jnp.dot(xt[...], g_all[:, where], preferred_element_type=F32).astype(BF16)

    total = ghp[at(z, hrows), :].astype(F32)
    for dz in range(1, Z):
        source = lax.rem(z + dz, Z)
        remote(
            ghp.at[at(source, hrows)], gh_rx.at[source], gh_send.at[0], gh_recv.at[source], (t, c, source)
        ).wait_recv()
        total = total + gh_rx[source].astype(F32)
    gh_ref[...] = total.astype(BF16)

    for target, copy in gh_out:
        @pl.when(target != z)
        def _(copy=copy):
            copy.wait_send()
    for copy in sent + st_out + s_first + s_second + t_first + t_second:
        copy.wait_send()
    for j in ORDER:
        tpair[j].wait_send()
    for step in range(Z - 1):
        z_end(step)


def shards(teacher_of_seq, teacher_hidden, teacher_weight, student_hidden, student_weight):
    Z = lax.axis_size("vocab")
    owners = lax.axis_size("teacher") * lax.axis_size("dp")
    cols = student_weight.shape[1]
    row_count, features = student_hidden.shape
    rows = row_count // owners
    seqs = teacher_of_seq.shape[0]
    positions = row_count // seqs
    ids = jnp.arange(seqs, dtype=jnp.int32)
    same = (teacher_of_seq[None, :] == teacher_of_seq[:, None]) & (ids[None, :] < ids[:, None])
    zrows, width = teacher_hidden.shape[1:]
    all_rows = jnp.arange(row_count, dtype=jnp.int32)
    slot = jnp.repeat(jnp.sum(same.astype(jnp.int32), axis=1), positions) * positions + all_rows % positions
    live = jnp.repeat(teacher_of_seq == lax.axis_index("teacher"), positions)
    slot_ids = jnp.arange(zrows * Z, dtype=jnp.int32)
    pick = ((slot[:, None] == slot_ids[None, :]) & live[:, None]).astype(BF16)
    hrows = row_count // Z
    dma = pltpu.SemaphoreType.DMA
    vmem = pl.BlockSpec(memory_space=pltpu.VMEM)
    hop_sems = [dma((4,)), dma((4,)), dma((2, 2)), dma((2, 2)), dma((2,)), dma((2,))]
    kl, grad_weight, grad_hidden = pl.pallas_call(
        functools.partial(kernel, Z, float(cols * Z)),
        out_shape=(
            jax.ShapeDtypeStruct((8, rows), F32),
            jax.ShapeDtypeStruct((features, cols), BF16),
            jax.ShapeDtypeStruct((hrows, features), BF16),
        ),
        in_specs=[vmem, vmem, pl.BlockSpec(memory_space=pl.ANY), vmem, vmem],
        out_specs=(vmem, vmem, vmem),
        scratch_shapes=[
            pltpu.VMEM((width, cols), BF16),
            pltpu.VMEM((zrows * Z, width), BF16),
            pltpu.VMEM((2 * rows, width), BF16),
            pltpu.VMEM((4, 2, rows, cols), F32),
            pltpu.VMEM((4, rows, cols), F32),
            pltpu.VMEM((2, rows, cols), F32),
            pltpu.VMEM((rows, cols), F32),
            pltpu.VMEM((4, rows, cols), F32),
            pltpu.VMEM((4, rows, cols), BF16),
            pltpu.VMEM((2, rows, cols), BF16),
            pltpu.VMEM((rows, cols), BF16),
            pltpu.VMEM((features, row_count), BF16),
            pltpu.VMEM((Z, 8, rows), F32),
            pltpu.VMEM((rows, rows), F32),
            pltpu.VMEM((row_count, cols), BF16),
            pltpu.VMEM((row_count, features), BF16),
            pltpu.VMEM((Z, hrows, features), BF16),
            dma(()), dma((2, Z)), dma((Z,)),
            *hop_sems, *hop_sems,
            dma((Z,)), dma((Z,)), dma((4,)), dma((4,)), dma((4,)), dma((4,)), dma((Z,)), dma((Z,)),
        ],
        compiler_params=pltpu.CompilerParams(
            collective_id=0, has_side_effects=True, vmem_limit_bytes=60 * 1024 * 1024
        ),
    )(pick, teacher_hidden[0], teacher_weight[0], student_hidden, student_weight)
    return (kl[0], grad_weight, grad_hidden)


def solution(mesh):
    in_specs = (
        P(),
        P("teacher", "vocab", "dp"),
        P("teacher", "dp", "vocab"),
        P(None, ("teacher", "dp")),
        P(("teacher", "dp"), "vocab"),
    )
    out_specs = (P(("teacher", "dp")), P(("teacher", "dp"), "vocab"), P("vocab", ("teacher", "dp")))
    return jax.shard_map(shards, mesh=mesh, in_specs=in_specs, out_specs=out_specs, check_vma=False)
```

```python
import functools

import jax
import jax.numpy as jnp
from jax import lax
from jax.experimental import pallas as pl
from jax.experimental.pallas import tpu as pltpu
from jax.sharding import PartitionSpec as P

MESH = pl.DeviceIdType.MESH
F32 = jnp.float32
BF16 = jnp.bfloat16


def kernel(
    Z, vocab_total,
    pick_ref, hidden_ref, head_ref, x_ref, w_ref,
    kl_ref, gw_ref, gh_ref,
    head, th, ph, work, s_rx, s_r1, s_r2, t_rx, t_sum, t_r1, t_r2, xp, xt, kl_mine, kl_all, st, tile, g_all, ghp, gh_rx,
    head_sem, z_send, z_recv,
    sc_send, sc_recv, s1_send, s1_recv, s2_send, s2_recv,
    tc_send, tc_recv, t1_send, t1_recv, t2_send, t2_recv,
    st_send, st_recv, g_send, g_recv, gc_send, gc_recv, gh_send, gh_recv, kl_send, kl_recv,
):
    t = lax.axis_index("teacher")
    c = lax.axis_index("dp")
    z = lax.axis_index("vocab")
    low = lax.rem(t, 2)
    high = lax.div(t, 2)
    mates = (t, t + 1 - 2 * low, t + 2 - 4 * high, 3 - t)
    other = 1 - c
    devs = tuple((m, c, z) for m in mates)
    core = (t, other, z)
    rows, cols = s_r2.shape
    half = cols // 2
    cut = (pl.ds(0, half), pl.ds(half, half))
    zrows = hidden_ref.shape[0]
    hrows = gh_ref.shape[0]
    unit = rows // 4
    piece = min(2 * unit, hrows)
    mine_at = 2 * low + c

    def at(block, count):
        return pl.ds(pl.multiple_of(block * count, count), count)

    def remote(src, dst, send, recv, dev):
        return pltpu.make_async_remote_copy(
            src_ref=src, dst_ref=dst, send_sem=send, recv_sem=recv, device_id=dev, device_id_type=MESH
        )

    barrier = pltpu.get_barrier_semaphore()
    for dev in (core, *devs[1:], *((m, other, z) for m in mates[1:])):
        pl.semaphore_signal(barrier, inc=1, device_id=dev, device_id_type=MESH)
    for dz in range(1, Z):
        pl.semaphore_signal(barrier, inc=1, device_id=(t, c, lax.rem(z + dz, Z)), device_id_type=MESH)
    head_copy = pltpu.make_async_copy(head_ref, head, head_sem)
    head_copy.start()
    th[at(z, zrows), :] = hidden_ref[...]
    pl.semaphore_wait(barrier, 6 + Z)

    def z_copy(block, way, step, target):
        return remote(
            th.at[at(block, zrows)], th.at[at(block, zrows)], z_send.at[way, step], z_recv.at[block], (t, c, target)
        )

    def z_start(step):
        @pl.when((z - step >= 0) & (z + 1 < Z))
        def _():
            z_copy(z - step, 0, step, z + 1).start()

        @pl.when((z + step < Z) & (z >= 1))
        def _():
            z_copy(z + step, 1, step, z - 1).start()

    def z_wait(step):
        @pl.when(z - 1 - step >= 0)
        def _():
            z_copy(z - 1 - step, 0, step, z - 1).wait_recv()

        @pl.when(z + 1 + step < Z)
        def _():
            z_copy(z + 1 + step, 1, step, z + 1).wait_recv()

    def z_end(step):
        @pl.when((z - step >= 0) & (z + 1 < Z))
        def _():
            z_copy(z - step, 0, step, z + 1).wait_send()

        @pl.when((z + step < Z) & (z >= 1))
        def _():
            z_copy(z + step, 1, step, z - 1).wait_send()

    def owner(j, which):
        return 2 * mates[j] + which

    def first_hop(j, summed, r1, sems):
        send, recv = sems
        copies = []
        if j == 3:
            for h in (0, 1):
                copies.append(
                    remote(summed.at[3, :, cut[h]], r1.at[0, :, cut[h]], send.at[0, h], recv.at[0, h], devs[1 + h])
                )
        elif j in (1, 2):
            h = j - 1
            copies.append(
                remote(summed.at[j, :, cut[h]], r1.at[1, :, cut[h]], send.at[1, h], recv.at[1, h], devs[j])
            )
        for copy in copies:
            copy.start()
        return copies

    def second_hop(h, first, summed, r1, r2, sems):
        send, recv = sems
        j = 2 - h
        first[h].wait_recv()
        summed[j, :, cut[h]] = (
            summed[j, :, cut[h]].astype(F32) + r1[0, :, cut[h]].astype(F32)
        ).astype(summed.dtype)
        copy = remote(summed.at[j, :, cut[h]], r2.at[:, cut[h]], send.at[h], recv.at[h], devs[j])
        copy.start()
        return copy

    ORDER = (3, 1, 2, 0)
    z_start(0)
    for o in range(8):
        for q in range(4):
            xp[o * rows + q * unit:o * rows + (q + 1) * unit, :] = x_ref[
                (q * 8 + o) * unit:(q * 8 + o + 1) * unit, :
            ]
    pair = {}
    for j in ORDER:
        work[j, other] = jnp.dot(xp[at(owner(j, other), rows), :], w_ref[...], preferred_element_type=F32)
        pair[j] = remote(work.at[j, other], s_rx.at[j], sc_send.at[j], sc_recv.at[j], core)
        pair[j].start()
    s_first = []
    for j in ORDER:
        mine = jnp.dot(xp[at(owner(j, c), rows), :], w_ref[...], preferred_element_type=F32)
        pair[j].wait_recv()
        s_rx[j] = s_rx[j] + mine
        s_first += first_hop(j, s_rx, s_r1, (s1_send, s1_recv))
    xt[...] = xp[...].T
    for step in range(Z - 1):
        z_wait(step)
        if step + 1 < Z - 1:
            z_start(step + 1)
        if step == 0:
            s_second = [second_hop(h, s_first, s_rx, s_r1, s_r2, (s2_send, s2_recv)) for h in (0, 1)]
    head_copy.wait()

    for j in ORDER:
        pair[j].wait_send()
    chunk = cols // 8
    tpair = {}
    t_first = []

    def teacher_rows(j):
        tpair[j].wait_recv()
        t_sum[j] = (t_rx[j] + work[j, c]).astype(BF16)
        return first_hop(j, t_sum, t_r1, (t1_send, t1_recv))

    for n, j in enumerate(ORDER):
        ph[...] = jnp.dot(
            pick_ref[at(mates[j], 2 * rows), :], th[...], preferred_element_type=F32
        ).astype(BF16)

        @pl.loop(0, 8)
        def _(i, j=j):
            where = at(i, chunk)
            part = jnp.dot(ph[...], head[:, where], preferred_element_type=F32)
            work[j, 0, :, where] = part[:rows]
            work[j, 1, :, where] = part[rows:]

        tpair[j] = remote(work.at[j, other], t_rx.at[j], tc_send.at[j], tc_recv.at[j], core)
        tpair[j].start()
        if n:
            t_first += teacher_rows(ORDER[n - 1])
    t_first += teacher_rows(ORDER[-1])
    t_second = [second_hop(h, t_first, t_sum, t_r1, t_r2, (t2_send, t2_recv)) for h in (0, 1)]

    s_first[2].wait_recv()
    s_first[3].wait_recv()
    for h in (0, 1):
        s_second[h].wait_recv()
    s_rx[0] = s_rx[0] + s_r1[1] + s_r2[...]
    student = s_rx[0]
    s_top = jnp.max(student, axis=1, keepdims=True)
    s_total = jnp.sum(jnp.exp(student - s_top), axis=1, keepdims=True)
    t_first[2].wait_recv()
    t_first[3].wait_recv()
    for h in (0, 1):
        t_second[h].wait_recv()
    t_sum[0] = (t_sum[0].astype(F32) + t_r1[1].astype(F32) + t_r2[...].astype(F32)).astype(BF16)
    teacher = t_sum[0].astype(F32)
    t_top = jnp.max(teacher, axis=1, keepdims=True)
    t_exp = jnp.exp(teacher - t_top)
    t_total = jnp.sum(t_exp, axis=1, keepdims=True)
    cross = jnp.sum(t_exp * (teacher - s_rx[0]), axis=1, keepdims=True)
    lane = lax.broadcasted_iota(jnp.int32, tile.shape, 1)
    packed = jnp.zeros(tile.shape, F32)
    for k, column in enumerate((t_top, t_total, s_top, s_total, cross)):
        packed = jnp.where(lane == k, column, packed)
    st[z] = packed.T[:8, :]
    st_out = []
    for dz in range(1, Z):
        copy = remote(st.at[z], st.at[z], st_send.at[dz], st_recv.at[z], (t, c, lax.rem(z + dz, Z)))
        copy.start()
        st_out.append(copy)
    for dz in range(1, Z):
        source = lax.rem(z + dz, Z)
        remote(st.at[source], st.at[source], st_send.at[dz], st_recv.at[source], (t, c, source)).wait_recv()
    every = [st[k] for k in range(Z)]
    t_top = functools.reduce(jnp.maximum, [e[0:1] for e in every])
    s_top = functools.reduce(jnp.maximum, [e[2:3] for e in every])
    t_total = sum(e[1:2] * jnp.exp(e[0:1] - t_top) for e in every)
    s_total = sum(e[3:4] * jnp.exp(e[2:3] - s_top) for e in every)
    t_lse = t_top + jnp.log(t_total)
    s_lse = s_top + jnp.log(s_total)
    cross = sum(e[4:5] * jnp.exp(e[0:1] - t_lse) for e in every)
    kl = cross - t_lse + s_lse
    line = lax.broadcasted_iota(jnp.int32, tile.shape, 0)
    tile[...] = jnp.where(line == 0, t_lse, jnp.where(line == 1, s_lse, 0.0)).T
    kl_mine[...] = jnp.broadcast_to(kl, tile.shape).T
    t_lse = tile[:, 0:1]
    s_lse = tile[:, 1:2]
    me = owner(0, c)
    g_all[at(me, rows), :] = (
        vocab_total * (jnp.exp(s_rx[0] - s_lse) - jnp.exp(t_sum[0].astype(F32) - t_lse))
    ).astype(BF16)

    def g_copy(j, which, sems, k, dev, columns=pl.ds(0, cols)):
        ref = g_all.at[at(owner(j, which), rows), columns]
        return remote(ref, ref, sems[0].at[k], sems[1].at[k], dev)

    chips, cores = (g_send, g_recv), (gc_send, gc_recv)
    sent = [g_copy(0, c, chips, 0, devs[1]), g_copy(0, c, chips, 1, devs[2]), g_copy(0, c, cores, 0, core)]
    for copy in sent:
        copy.start()

    def kl_copy(j):
        return remote(
            kl_mine.at[at(mates[j], unit), :], kl_all.at[at(mine_at, unit), :],
            kl_send.at[j], kl_recv.at[mine_at], (mates[j], high, z),
        )

    @pl.when(high != c)
    def _():
        kl_copy(0).start()

    @pl.when(high == c)
    def _():
        kl_all[at(mine_at, unit), :] = kl_mine[at(t, unit), :]

    for j in (1, 2, 3):
        kl_copy(j).start()

    def arrived(j, k, columns=pl.ds(0, cols)):
        g_copy(j, c, chips, k, devs[1], columns).wait_recv()

    def forward(j, sems, k, dev, columns=pl.ds(0, cols)):
        copy = g_copy(j, c, sems, k, dev, columns)
        copy.start()
        sent.append(copy)

    gh_out = []

    def hidden_rows(j):
        g_copy(j, other, cores, j, core).wait_recv()
        where = at(mates[j], 2 * rows)
        part = lax.dot_general(
            g_all[where, :], w_ref[...], (((1,), (1,)), ((), ())), preferred_element_type=F32
        ).astype(BF16)
        for q in range(4):
            for k in (0, 1):
                ghp[at(q * 8 + 2 * mates[j] + k, unit), :] = part[k * rows + q * unit:k * rows + (q + 1) * unit]
            for p in range(2 * unit // piece):
                first = q * 8 * unit + mates[j] * 2 * unit + p * piece
                target, inside = lax.div(first, hrows), lax.div(lax.rem(first, hrows), piece)
                copy = remote(
                    ghp.at[at(lax.div(first, piece), piece)], gh_rx.at[z, at(inside, piece)],
                    gh_send.at[len(gh_out)], gh_recv.at[z, inside], (t, c, target),
                )
                gh_out.append((target, copy))

                @pl.when(target != z)
                def _(copy=copy):
                    copy.start()

    arrived(1, 0)
    forward(1, chips, 2, devs[2], cut[0])
    forward(1, cores, 1, core)
    arrived(2, 1)
    forward(2, chips, 3, devs[1], cut[1])
    forward(2, cores, 2, core)
    hidden_rows(0)
    hidden_rows(1)
    hidden_rows(2)
    arrived(3, 2, cut[0])
    arrived(3, 3, cut[1])
    forward(3, cores, 3, core)
    hidden_rows(3)

    wide = cols // 4
    @pl.loop(0, 4)
    def _(i):
        where = at(i, wide)
        gw_ref[:, where] = jnp.dot(xt[...], g_all[:, where], preferred_element_type=F32).astype(BF16)

    total = ghp[at(z, hrows), :].astype(F32)
    for dz in range(1, Z):
        source = lax.rem(z + dz, Z)
        for p in range(hrows // piece):
            where = pl.ds(p * piece, piece)
            remote(
                ghp.at[where], gh_rx.at[source, where], gh_send.at[0], gh_recv.at[source, p], (t, c, source)
            ).wait_recv()
        total = total + gh_rx[source].astype(F32)
    gh_ref[...] = total.astype(BF16)

    for k in range(4):
        here = (2 * c + k // 2 == t) & (c == k % 2)

        @pl.when(jnp.logical_not(here))
        def _(k=k):
            where = pl.ds(k * unit, unit)
            remote(
                kl_mine.at[where, :], kl_all.at[where, :], kl_send.at[0], kl_recv.at[k], core
            ).wait_recv()

    kl_ref[...] = kl_all[...].T[:8, :]

    @pl.when(high != c)
    def _():
        kl_copy(0).wait_send()

    for j in (1, 2, 3):
        kl_copy(j).wait_send()
    for target, copy in gh_out:
        @pl.when(target != z)
        def _(copy=copy):
            copy.wait_send()
    for copy in sent + st_out + s_first + s_second + t_first + t_second:
        copy.wait_send()
    for j in ORDER:
        tpair[j].wait_send()
    for step in range(Z - 1):
        z_end(step)


def shards(teacher_of_seq, teacher_hidden, teacher_weight, student_hidden, student_weight):
    Z = lax.axis_size("vocab")
    owners = lax.axis_size("teacher") * lax.axis_size("dp")
    cols = student_weight.shape[1]
    row_count, features = student_hidden.shape
    rows = row_count // owners
    seqs = teacher_of_seq.shape[0]
    positions = row_count // seqs
    ids = jnp.arange(seqs, dtype=jnp.int32)
    same = (teacher_of_seq[None, :] == teacher_of_seq[:, None]) & (ids[None, :] < ids[:, None])
    zrows, width = teacher_hidden.shape[1:]
    unit = rows // 4
    piece = min(2 * unit, row_count // Z)
    all_rows = jnp.arange(row_count, dtype=jnp.int32).reshape(4, owners, unit)
    all_rows = all_rows.transpose(1, 0, 2).reshape(row_count)
    sequence = all_rows // positions
    chosen = sequence[:, None] == ids[None, :]
    earlier = jnp.sum(same.astype(jnp.int32), axis=1)
    slot = jnp.sum(jnp.where(chosen, earlier[None, :], 0), axis=1) * positions + all_rows % positions
    live = jnp.any(chosen & (teacher_of_seq == lax.axis_index("teacher"))[None, :], axis=1)
    slot_ids = jnp.arange(zrows * Z, dtype=jnp.int32)
    pick = ((slot[:, None] == slot_ids[None, :]) & live[:, None]).astype(BF16)
    hrows = row_count // Z
    dma = pltpu.SemaphoreType.DMA
    vmem = pl.BlockSpec(memory_space=pltpu.VMEM)
    hop_sems = [dma((4,)), dma((4,)), dma((2, 2)), dma((2, 2)), dma((2,)), dma((2,))]
    kl, grad_weight, grad_hidden = pl.pallas_call(
        functools.partial(kernel, Z, float(cols * Z)),
        out_shape=(
            jax.ShapeDtypeStruct((8, rows), F32),
            jax.ShapeDtypeStruct((features, cols), BF16),
            jax.ShapeDtypeStruct((hrows, features), BF16),
        ),
        in_specs=[vmem, vmem, pl.BlockSpec(memory_space=pl.ANY), vmem, vmem],
        out_specs=(vmem, vmem, vmem),
        scratch_shapes=[
            pltpu.VMEM((width, cols), BF16),
            pltpu.VMEM((zrows * Z, width), BF16),
            pltpu.VMEM((2 * rows, width), BF16),
            pltpu.VMEM((4, 2, rows, cols), F32),
            pltpu.VMEM((4, rows, cols), F32),
            pltpu.VMEM((2, rows, cols), F32),
            pltpu.VMEM((rows, cols), F32),
            pltpu.VMEM((4, rows, cols), F32),
            pltpu.VMEM((4, rows, cols), BF16),
            pltpu.VMEM((2, rows, cols), BF16),
            pltpu.VMEM((rows, cols), BF16),
            pltpu.VMEM((row_count, features), BF16),
            pltpu.VMEM((features, row_count), BF16),
            pltpu.VMEM((rows, rows), F32),
            pltpu.VMEM((rows, rows), F32),
            pltpu.VMEM((Z, 8, rows), F32),
            pltpu.VMEM((rows, rows), F32),
            pltpu.VMEM((row_count, cols), BF16),
            pltpu.VMEM((row_count, features), BF16),
            pltpu.VMEM((Z, hrows, features), BF16),
            dma(()), dma((2, Z)), dma((Z,)),
            *hop_sems, *hop_sems,
            dma((Z,)), dma((Z,)), dma((4,)), dma((4,)), dma((4,)), dma((4,)),
            dma((row_count // piece,)), dma((Z, hrows // piece)), dma((4,)), dma((4,)),
        ],
        compiler_params=pltpu.CompilerParams(
            collective_id=0, has_side_effects=True, vmem_limit_bytes=60 * 1024 * 1024
        ),
    )(pick, teacher_hidden[0], teacher_weight[0], student_hidden, student_weight)
    return (kl[0], grad_weight, grad_hidden)


def solution(mesh):
    in_specs = (
        P(),
        P("teacher", "vocab", "dp"),
        P("teacher", "dp", "vocab"),
        P(None, ("teacher", "dp")),
        P(("teacher", "dp"), "vocab"),
    )
    out_specs = (P(("teacher", "dp")), P(("teacher", "dp"), "vocab"), P("vocab", ("teacher", "dp")))
    return jax.shard_map(shards, mesh=mesh, in_specs=in_specs, out_specs=out_specs, check_vma=False)
```

```python
import functools

import jax
import jax.numpy as jnp
from jax import lax
from jax.experimental import pallas as pl
from jax.experimental.pallas import tpu as pltpu
from jax.sharding import PartitionSpec as P

MESH = pl.DeviceIdType.MESH
F32 = jnp.float32
BF16 = jnp.bfloat16


def kernel(
    Z, vocab_total,
    pick_ref, hidden_ref, head_ref, x_ref, w_ref,
    kl_ref, gw_ref, gh_ref,
    head, th, ph, work, s_rx, s_r1, s_r2, t_rx, t_sum, t_r1, t_r2, xp, xt, kl_mine, kl_all, st, tile, g_all, ghp, gh_rx,
    head_sem, z_send, z_recv,
    sc_send, sc_recv, s1_send, s1_recv, s2_send, s2_recv,
    tc_send, tc_recv, t1_send, t1_recv, t2_send, t2_recv,
    st_send, st_recv, g_send, g_recv, gc_send, gc_recv, gh_send, gh_recv, kl_send, kl_recv,
):
    t = lax.axis_index("teacher")
    c = lax.axis_index("dp")
    z = lax.axis_index("vocab")
    low = lax.rem(t, 2)
    high = lax.div(t, 2)
    mates = (t, t + 1 - 2 * low, t + 2 - 4 * high, 3 - t)
    other = 1 - c
    devs = tuple((m, c, z) for m in mates)
    core = (t, other, z)
    rows, cols = s_r2.shape
    half = cols // 2
    cut = (pl.ds(0, half), pl.ds(half, half))
    zrows = hidden_ref.shape[0]
    hrows = gh_ref.shape[0]
    unit = rows // 4
    piece = min(2 * unit, hrows)
    mine_at = 2 * low + c

    def at(block, count):
        return pl.ds(pl.multiple_of(block * count, count), count)

    def remote(src, dst, send, recv, dev):
        return pltpu.make_async_remote_copy(
            src_ref=src, dst_ref=dst, send_sem=send, recv_sem=recv, device_id=dev, device_id_type=MESH
        )

    barrier = pltpu.get_barrier_semaphore()
    for dev in (core, *devs[1:], *((m, other, z) for m in mates[1:])):
        pl.semaphore_signal(barrier, inc=1, device_id=dev, device_id_type=MESH)
    for dz in range(1, Z):
        pl.semaphore_signal(barrier, inc=1, device_id=(t, c, lax.rem(z + dz, Z)), device_id_type=MESH)
    head_copy = pltpu.make_async_copy(head_ref, head, head_sem)
    head_copy.start()
    th[at(z, zrows), :] = hidden_ref[...]
    pl.semaphore_wait(barrier, 6 + Z)

    def z_copy(block, way, step, target):
        return remote(
            th.at[at(block, zrows)], th.at[at(block, zrows)], z_send.at[way, step], z_recv.at[block], (t, c, target)
        )

    def z_start(step):
        @pl.when((z - step >= 0) & (z + 1 < Z))
        def _():
            z_copy(z - step, 0, step, z + 1).start()

        @pl.when((z + step < Z) & (z >= 1))
        def _():
            z_copy(z + step, 1, step, z - 1).start()

    def z_wait(step):
        @pl.when(z - 1 - step >= 0)
        def _():
            z_copy(z - 1 - step, 0, step, z - 1).wait_recv()

        @pl.when(z + 1 + step < Z)
        def _():
            z_copy(z + 1 + step, 1, step, z + 1).wait_recv()

    def z_end(step):
        @pl.when((z - step >= 0) & (z + 1 < Z))
        def _():
            z_copy(z - step, 0, step, z + 1).wait_send()

        @pl.when((z + step < Z) & (z >= 1))
        def _():
            z_copy(z + step, 1, step, z - 1).wait_send()

    def owner(j, which):
        return 2 * mates[j] + which

    def first_hop(j, summed, r1, sems):
        send, recv = sems
        copies = []
        if j == 3:
            for h in (0, 1):
                copies.append(
                    remote(summed.at[3, :, cut[h]], r1.at[0, :, cut[h]], send.at[0, h], recv.at[0, h], devs[1 + h])
                )
        elif j in (1, 2):
            h = j - 1
            copies.append(
                remote(summed.at[j, :, cut[h]], r1.at[1, :, cut[h]], send.at[1, h], recv.at[1, h], devs[j])
            )
        for copy in copies:
            copy.start()
        return copies

    def second_hop(h, first, summed, r1, r2, sems):
        send, recv = sems
        j = 2 - h
        first[h].wait_recv()
        summed[j, :, cut[h]] = (
            summed[j, :, cut[h]].astype(F32) + r1[0, :, cut[h]].astype(F32)
        ).astype(summed.dtype)
        copy = remote(summed.at[j, :, cut[h]], r2.at[:, cut[h]], send.at[h], recv.at[h], devs[j])
        copy.start()
        return copy

    ORDER = (3, 1, 2, 0)
    z_start(0)
    for o in range(8):
        for q in range(4):
            xp[o * rows + q * unit:o * rows + (q + 1) * unit, :] = x_ref[
                (q * 8 + o) * unit:(q * 8 + o + 1) * unit, :
            ]
    pair = {}
    for j in ORDER:
        work[j, other] = jnp.dot(xp[at(owner(j, other), rows), :], w_ref[...], preferred_element_type=F32)
        pair[j] = remote(work.at[j, other], s_rx.at[j], sc_send.at[j], sc_recv.at[j], core)
        pair[j].start()
    s_first = []
    for n, j in enumerate(ORDER):
        if n == 3:
            z_wait(0)
            z_start(1)
        mine = jnp.dot(xp[at(owner(j, c), rows), :], w_ref[...], preferred_element_type=F32)
        pair[j].wait_recv()
        s_rx[j] = s_rx[j] + mine
        s_first += first_hop(j, s_rx, s_r1, (s1_send, s1_recv))
    s_second = [second_hop(h, s_first, s_rx, s_r1, s_r2, (s2_send, s2_recv)) for h in (0, 1)]
    for step in range(1, Z - 1):
        z_wait(step)
        if step + 1 < Z - 1:
            z_start(step + 1)
        if step == 1:
            xt[...] = xp[...].T
    head_copy.wait()

    for j in ORDER:
        pair[j].wait_send()
    chunk = cols // 8
    tpair = {}
    t_first = []

    def teacher_rows(j):
        tpair[j].wait_recv()
        t_sum[j] = (t_rx[j] + work[j, c]).astype(BF16)
        return first_hop(j, t_sum, t_r1, (t1_send, t1_recv))

    for n, j in enumerate(ORDER):
        ph[...] = jnp.dot(
            pick_ref[at(mates[j], 2 * rows), :], th[...], preferred_element_type=F32
        ).astype(BF16)

        @pl.loop(0, 8)
        def _(i, j=j):
            where = at(i, chunk)
            part = jnp.dot(ph[...], head[:, where], preferred_element_type=F32)
            work[j, 0, :, where] = part[:rows]
            work[j, 1, :, where] = part[rows:]

        tpair[j] = remote(work.at[j, other], t_rx.at[j], tc_send.at[j], tc_recv.at[j], core)
        tpair[j].start()
        if n:
            t_first += teacher_rows(ORDER[n - 1])
    t_first += teacher_rows(ORDER[-1])
    t_second = [second_hop(h, t_first, t_sum, t_r1, t_r2, (t2_send, t2_recv)) for h in (0, 1)]

    s_first[2].wait_recv()
    s_first[3].wait_recv()
    for h in (0, 1):
        s_second[h].wait_recv()
    s_rx[0] = s_rx[0] + s_r1[1] + s_r2[...]
    student = s_rx[0]
    s_top = jnp.max(student, axis=1, keepdims=True)
    s_total = jnp.sum(jnp.exp(student - s_top), axis=1, keepdims=True)
    t_first[2].wait_recv()
    t_first[3].wait_recv()
    for h in (0, 1):
        t_second[h].wait_recv()
    t_sum[0] = (t_sum[0].astype(F32) + t_r1[1].astype(F32) + t_r2[...].astype(F32)).astype(BF16)
    teacher = t_sum[0].astype(F32)
    t_top = jnp.max(teacher, axis=1, keepdims=True)
    t_exp = jnp.exp(teacher - t_top)
    t_total = jnp.sum(t_exp, axis=1, keepdims=True)
    cross = jnp.sum(t_exp * (teacher - s_rx[0]), axis=1, keepdims=True)
    lane = lax.broadcasted_iota(jnp.int32, tile.shape, 1)
    packed = jnp.zeros(tile.shape, F32)
    for k, column in enumerate((t_top, t_total, s_top, s_total, cross)):
        packed = jnp.where(lane == k, column, packed)
    st[z] = packed.T[:8, :]
    st_out = []
    for dz in range(1, Z):
        copy = remote(st.at[z], st.at[z], st_send.at[dz], st_recv.at[z], (t, c, lax.rem(z + dz, Z)))
        copy.start()
        st_out.append(copy)
    for dz in range(1, Z):
        source = lax.rem(z + dz, Z)
        remote(st.at[source], st.at[source], st_send.at[dz], st_recv.at[source], (t, c, source)).wait_recv()
    every = [st[k] for k in range(Z)]
    t_top = functools.reduce(jnp.maximum, [e[0:1] for e in every])
    s_top = functools.reduce(jnp.maximum, [e[2:3] for e in every])
    t_total = sum(e[1:2] * jnp.exp(e[0:1] - t_top) for e in every)
    s_total = sum(e[3:4] * jnp.exp(e[2:3] - s_top) for e in every)
    t_lse = t_top + jnp.log(t_total)
    s_lse = s_top + jnp.log(s_total)
    cross = sum(e[4:5] * jnp.exp(e[0:1] - t_lse) for e in every)
    kl = cross - t_lse + s_lse
    line = lax.broadcasted_iota(jnp.int32, tile.shape, 0)
    tile[...] = jnp.where(line == 0, t_lse, jnp.where(line == 1, s_lse, 0.0)).T
    kl_mine[...] = jnp.broadcast_to(kl, tile.shape).T
    t_lse = tile[:, 0:1]
    s_lse = tile[:, 1:2]
    me = owner(0, c)
    g_all[at(me, rows), :] = (
        vocab_total * (jnp.exp(s_rx[0] - s_lse) - jnp.exp(t_sum[0].astype(F32) - t_lse))
    ).astype(BF16)

    def g_copy(j, which, sems, k, dev, columns=pl.ds(0, cols)):
        ref = g_all.at[at(owner(j, which), rows), columns]
        return remote(ref, ref, sems[0].at[k], sems[1].at[k], dev)

    chips, cores = (g_send, g_recv), (gc_send, gc_recv)
    sent = [g_copy(0, c, chips, 0, devs[1]), g_copy(0, c, chips, 1, devs[2]), g_copy(0, c, cores, 0, core)]
    for copy in sent:
        copy.start()

    def kl_copy(j):
        return remote(
            kl_mine.at[at(mates[j], unit), :], kl_all.at[at(mine_at, unit), :],
            kl_send.at[j], kl_recv.at[mine_at], (mates[j], high, z),
        )

    @pl.when(high != c)
    def _():
        kl_copy(0).start()

    @pl.when(high == c)
    def _():
        kl_all[at(mine_at, unit), :] = kl_mine[at(t, unit), :]

    for j in (1, 2, 3):
        kl_copy(j).start()

    def arrived(j, k, columns=pl.ds(0, cols)):
        g_copy(j, c, chips, k, devs[1], columns).wait_recv()

    def forward(j, sems, k, dev, columns=pl.ds(0, cols)):
        copy = g_copy(j, c, sems, k, dev, columns)
        copy.start()
        sent.append(copy)

    gh_out = []

    def hidden_rows(j):
        g_copy(j, other, cores, j, core).wait_recv()
        where = at(mates[j], 2 * rows)
        part = lax.dot_general(
            g_all[where, :], w_ref[...], (((1,), (1,)), ((), ())), preferred_element_type=F32
        ).astype(BF16)
        for q in range(4):
            for k in (0, 1):
                ghp[at(q * 8 + 2 * mates[j] + k, unit), :] = part[k * rows + q * unit:k * rows + (q + 1) * unit]
            for p in range(2 * unit // piece):
                first = q * 8 * unit + mates[j] * 2 * unit + p * piece
                target, inside = lax.div(first, hrows), lax.div(lax.rem(first, hrows), piece)
                copy = remote(
                    ghp.at[at(lax.div(first, piece), piece)], gh_rx.at[z, at(inside, piece)],
                    gh_send.at[len(gh_out)], gh_recv.at[z, inside], (t, c, target),
                )
                gh_out.append((target, copy))

                @pl.when(target != z)
                def _(copy=copy):
                    copy.start()

    arrived(1, 0)
    forward(1, chips, 2, devs[2], cut[0])
    forward(1, cores, 1, core)
    arrived(2, 1)
    forward(2, chips, 3, devs[1], cut[1])
    forward(2, cores, 2, core)
    hidden_rows(0)
    hidden_rows(1)
    hidden_rows(2)
    arrived(3, 2, cut[0])
    arrived(3, 3, cut[1])
    forward(3, cores, 3, core)
    hidden_rows(3)

    wide = cols // 4
    @pl.loop(0, 4)
    def _(i):
        where = at(i, wide)
        gw_ref[:, where] = jnp.dot(xt[...], g_all[:, where], preferred_element_type=F32).astype(BF16)

    total = ghp[at(z, hrows), :].astype(F32)
    for dz in range(1, Z):
        source = lax.rem(z + dz, Z)
        for p in range(hrows // piece):
            where = pl.ds(p * piece, piece)
            remote(
                ghp.at[where], gh_rx.at[source, where], gh_send.at[0], gh_recv.at[source, p], (t, c, source)
            ).wait_recv()
        total = total + gh_rx[source].astype(F32)
    gh_ref[...] = total.astype(BF16)

    for k in range(4):
        here = (2 * c + k // 2 == t) & (c == k % 2)

        @pl.when(jnp.logical_not(here))
        def _(k=k):
            where = pl.ds(k * unit, unit)
            remote(
                kl_mine.at[where, :], kl_all.at[where, :], kl_send.at[0], kl_recv.at[k], core
            ).wait_recv()

    kl_ref[...] = kl_all[...].T[:8, :]

    @pl.when(high != c)
    def _():
        kl_copy(0).wait_send()

    for j in (1, 2, 3):
        kl_copy(j).wait_send()
    for target, copy in gh_out:
        @pl.when(target != z)
        def _(copy=copy):
            copy.wait_send()
    for copy in sent + st_out + s_first + s_second + t_first + t_second:
        copy.wait_send()
    for j in ORDER:
        tpair[j].wait_send()
    for step in range(Z - 1):
        z_end(step)


def shards(teacher_of_seq, teacher_hidden, teacher_weight, student_hidden, student_weight):
    Z = lax.axis_size("vocab")
    owners = lax.axis_size("teacher") * lax.axis_size("dp")
    cols = student_weight.shape[1]
    row_count, features = student_hidden.shape
    rows = row_count // owners
    seqs = teacher_of_seq.shape[0]
    positions = row_count // seqs
    ids = jnp.arange(seqs, dtype=jnp.int32)
    same = (teacher_of_seq[None, :] == teacher_of_seq[:, None]) & (ids[None, :] < ids[:, None])
    zrows, width = teacher_hidden.shape[1:]
    unit = rows // 4
    piece = min(2 * unit, row_count // Z)
    all_rows = jnp.arange(row_count, dtype=jnp.int32).reshape(4, owners, unit)
    all_rows = all_rows.transpose(1, 0, 2).reshape(row_count)
    sequence = all_rows // positions
    chosen = sequence[:, None] == ids[None, :]
    earlier = jnp.sum(same.astype(jnp.int32), axis=1)
    slot = jnp.sum(jnp.where(chosen, earlier[None, :], 0), axis=1) * positions + all_rows % positions
    live = jnp.any(chosen & (teacher_of_seq == lax.axis_index("teacher"))[None, :], axis=1)
    slot_ids = jnp.arange(zrows * Z, dtype=jnp.int32)
    pick = ((slot[:, None] == slot_ids[None, :]) & live[:, None]).astype(BF16)
    hrows = row_count // Z
    dma = pltpu.SemaphoreType.DMA
    vmem = pl.BlockSpec(memory_space=pltpu.VMEM)
    hop_sems = [dma((4,)), dma((4,)), dma((2, 2)), dma((2, 2)), dma((2,)), dma((2,))]
    kl, grad_weight, grad_hidden = pl.pallas_call(
        functools.partial(kernel, Z, float(cols * Z)),
        out_shape=(
            jax.ShapeDtypeStruct((8, rows), F32),
            jax.ShapeDtypeStruct((features, cols), BF16),
            jax.ShapeDtypeStruct((hrows, features), BF16),
        ),
        in_specs=[vmem, vmem, pl.BlockSpec(memory_space=pl.ANY), vmem, vmem],
        out_specs=(vmem, vmem, vmem),
        scratch_shapes=[
            pltpu.VMEM((width, cols), BF16),
            pltpu.VMEM((zrows * Z, width), BF16),
            pltpu.VMEM((2 * rows, width), BF16),
            pltpu.VMEM((4, 2, rows, cols), F32),
            pltpu.VMEM((4, rows, cols), F32),
            pltpu.VMEM((2, rows, cols), F32),
            pltpu.VMEM((rows, cols), F32),
            pltpu.VMEM((4, rows, cols), F32),
            pltpu.VMEM((4, rows, cols), BF16),
            pltpu.VMEM((2, rows, cols), BF16),
            pltpu.VMEM((rows, cols), BF16),
            pltpu.VMEM((row_count, features), BF16),
            pltpu.VMEM((features, row_count), BF16),
            pltpu.VMEM((rows, rows), F32),
            pltpu.VMEM((rows, rows), F32),
            pltpu.VMEM((Z, 8, rows), F32),
            pltpu.VMEM((rows, rows), F32),
            pltpu.VMEM((row_count, cols), BF16),
            pltpu.VMEM((row_count, features), BF16),
            pltpu.VMEM((Z, hrows, features), BF16),
            dma(()), dma((2, Z)), dma((Z,)),
            *hop_sems, *hop_sems,
            dma((Z,)), dma((Z,)), dma((4,)), dma((4,)), dma((4,)), dma((4,)),
            dma((row_count // piece,)), dma((Z, hrows // piece)), dma((4,)), dma((4,)),
        ],
        compiler_params=pltpu.CompilerParams(
            collective_id=0, has_side_effects=True, vmem_limit_bytes=60 * 1024 * 1024
        ),
    )(pick, teacher_hidden[0], teacher_weight[0], student_hidden, student_weight)
    return (kl[0], grad_weight, grad_hidden)


def solution(mesh):
    in_specs = (
        P(),
        P("teacher", "vocab", "dp"),
        P("teacher", "dp", "vocab"),
        P(None, ("teacher", "dp")),
        P(("teacher", "dp"), "vocab"),
    )
    out_specs = (P(("teacher", "dp")), P(("teacher", "dp"), "vocab"), P("vocab", ("teacher", "dp")))
    return jax.shard_map(shards, mesh=mesh, in_specs=in_specs, out_specs=out_specs, check_vma=False)
```
